32 devices in a mesh: rows: 8 (over z, y), rhs: 4 (over x, core).
Axes of the slice: x: 2, y: 2, z: 4, core: 2. Of those that a mesh axis runs over, the one named last changes fastest.
Arguments:
- kernel_rows: bfloat16 [16384, 512], P(('rows', 'rhs')), may hold values from 0 to 1
- factor_blocks: bfloat16 [64, 8, 256, 256], P('rows'), may hold values from -0.125 to 0.125
- diag_inverse: bfloat16 [64, 256, 256], P('rows'), as said below
- pattern: int32 [64, 8], P('rows'), may hold values from 0 to 63, as said below
- live_counts: int32 [64], P('rows'), may hold values from 0 to 8, as said below
Outputs:
- solution: bfloat16 [16384, 512], P('rows', 'rhs')
The draws below stay inside these ranges and needn't reach their ends.
Inputs may be any that keep to these rules, and one draw needn't show every extreme that they name: pattern[s, k] names a block row of a lower level than s; slot 0 of every block row above level 0 names a block row of the level just below; rows of level 0 hold 0. Block row t is held by index t // 8 of rows; the used slots of the block rows held by one index of rows name, for any one level, at most 2 distinct block rows held by any one other index. `live_counts`: 0 on level 0, from 1 to 8 on higher levels, 8 reached. `diag_inverse`: each block is the inverse of a well-conditioned diagonal block of the factor.
All inputs are finite; a program needn't handle non-finite values.
Results may differ from the reference program's by a relative error of at most 0.0058.
Values may be sent and summed in bfloat16 or wider, within the bound.
A program may use at most 128 MiB of HBM per device.

```python
import jax
import jax.numpy as jnp
import numpy as np
from jax import lax

BLK = 256
RHS = 512
LEV = 4
K = 8
BR_DEV = 2
NB = 64
N_ROWS = 8


def draw_pattern(key, part):
    per_device = LEV * BR_DEV
    total = LEV * BR_DEV * N_ROWS
    block_ids = jnp.arange(total)[:, None]
    level_of = block_ids % per_device // BR_DEV
    first_key, second_key, third_key = jax.random.split(jax.random.fold_in(key, 11), 3)
    picked = jax.random.randint(first_key, (total, K), 0, 420) % jnp.maximum(level_of, 1)
    slot_ids = jnp.arange(K)[None, :]
    source_level = jnp.where(slot_ids == 0, jnp.maximum(level_of - 1, 0), picked)
    orders = jax.random.permutation(second_key, jnp.tile(jnp.arange(N_ROWS)[None, :], (N_ROWS, 1)), axis=1, independent=True)
    owner = block_ids // per_device
    position = (block_ids % per_device * K + slot_ids) % N_ROWS
    source_holder = orders[owner, position]
    source_offset = jax.random.randint(third_key, (total, K), 0, BR_DEV)
    columns = source_holder * per_device + source_level * BR_DEV + source_offset
    return jnp.where(level_of > 0, columns, 0).astype(jnp.int32)


def draw_live_counts(key, part):
    per_device = LEV * BR_DEV
    total = LEV * BR_DEV * N_ROWS
    block_ids = jnp.arange(total)
    level_of = block_ids % per_device // BR_DEV
    counts = 1 + jax.random.randint(jax.random.fold_in(key, 23), (total,), 0, K)
    counts = jnp.where(block_ids == BR_DEV, K, counts)
    return jnp.where(level_of > 0, counts, 0).astype(jnp.int32)


def draw_diag_inverse(key, part):
    total = LEV * BR_DEV * N_ROWS
    first_key, second_key = jax.random.split(jax.random.fold_in(key, 37))
    scales = jax.random.uniform(first_key, (total, BLK), jnp.float32, 0.5, 1.5)
    spread = jax.random.normal(second_key, (total, BLK, BLK), jnp.float32) * (0.35 / BLK ** 0.5)
    eye_mask = jnp.eye(BLK, dtype=jnp.float32)[None, :, :]
    return (spread + eye_mask * scales[:, :, None]).astype(jnp.bfloat16)


def block_scale(key, shape, cuts, low, top_value):
    gain = 1.0
    for dim, blocks in cuts:
        heights = jax.random.uniform(jax.random.fold_in(jax.random.fold_in(key, 6), dim), (blocks,), jnp.float32, low / len(cuts), top_value / len(cuts))
        gain = gain * jnp.repeat(jnp.exp(heights), shape[dim] // blocks).reshape((-1,) + (1,) * (len(shape) - 1 - dim))
    return gain


def noise(own_key, extent, scale, bound, cuts=(), kind=jnp.bfloat16):
    values = jax.random.normal(own_key, extent, jnp.float32) * scale
    if len(cuts) > 0:
        values = block_scale(own_key, extent, cuts, -0.22, 0.18) * values
    return jnp.clip(values, min=-bound, max=bound).astype(kind)


def setup_inputs(seed: int = 0) -> dict:
    arg_keys = jax.random.split(jax.random.key(seed), 6)
    kernel_rows = jnp.clip(1.0 * jax.random.uniform(arg_keys[0], (NB * BLK, RHS), jnp.float32) ** block_scale(arg_keys[0], (NB * BLK, RHS), ((0, 32),), -0.2, 0.2), 0.0, 1.0).astype(jnp.bfloat16)
    factor_blocks = noise(arg_keys[1], (NB, K, BLK, BLK), (K * BLK) ** -0.5, 0.125, ((0, 8),))
    diag_inverse = draw_diag_inverse(jax.random.fold_in(arg_keys[5], 71), 0)
    pattern = draw_pattern(jax.random.fold_in(arg_keys[5], 71), 0)
    live_counts = draw_live_counts(jax.random.fold_in(arg_keys[5], 71), 0)
    return {"kernel_rows": kernel_rows, "factor_blocks": factor_blocks, "diag_inverse": diag_inverse, "pattern": pattern, "live_counts": live_counts}


def reference(kernel_rows, factor_blocks, diag_inverse, pattern, live_counts):
    per_device = LEV * BR_DEV
    right_side = kernel_rows.reshape(NB, BLK, RHS)
    solved = jnp.zeros((NB, BLK, RHS), jnp.bfloat16)
    slot_ids = jnp.arange(K)
    for level_now in range(LEV):
        members = np.array([holder * per_device + level_now * BR_DEV + offset for holder in range(N_ROWS) for offset in range(BR_DEV)], dtype=np.int32)

        def solve_one(member, solved=solved):
            columns = pattern[member]
            active = slot_ids < live_counts[member]
            blocks = jnp.take(solved, columns, axis=0, mode="clip")
            blocks = jnp.where(active[:, None, None], blocks, jnp.zeros_like(blocks))
            summed = jnp.einsum("kij,kjr->ir", factor_blocks[member].astype(jnp.float32), blocks.astype(jnp.float32))
            residual = (right_side[member].astype(jnp.float32) - summed).astype(jnp.bfloat16)
            return jnp.dot(diag_inverse[member], residual, preferred_element_type=jnp.float32).astype(jnp.bfloat16)

        newest = lax.map(solve_one, jnp.asarray(members))
        solved = solved.at[jnp.asarray(members)].set(newest)
    return solved.reshape(NB * BLK, RHS)
```

```python
import functools

import jax
import jax.numpy as jnp
from jax import lax
from jax.experimental import pallas as pl
from jax.experimental.pallas import tpu as pltpu
from jax.sharding import PartitionSpec as P

LEV = 4
MESH = pl.DeviceIdType.MESH


def kernel(rows, rhs, kr_hbm, fb_hbm, di_hbm, pat, live, out,
           right, factor, inverse, *rest):
    held = rest[: LEV - 1]
    fb_sem, di_sem, own_sem, kr_send, kr_recv, x_send, x_recv = rest[LEV - 1 :]
    per_device, slots, block, _ = fb_hbm.shape
    per_level = per_device // LEV
    width = out.shape[1]
    part = kr_hbm.shape[0]
    outer = rows // 2
    me_r = lax.axis_index("rows")
    me_h = lax.axis_index("rhs")
    z, y = me_r // 2, me_r % 2
    across = z * 2 + (1 - y)

    def line(d):
        return lax.rem(z + d, outer) * 2 + y

    fb_copies = []
    for lev in range(1, LEV):
        at = pl.ds(lev * per_level, per_level)
        fb_copies.append(pltpu.make_async_copy(
            fb_hbm.at[at], factor.at[pl.ds((lev - 1) * per_level, per_level)], fb_sem.at[lev - 1]))
    di_copy = pltpu.make_async_copy(di_hbm, inverse, di_sem)
    mine = pl.ds(pl.multiple_of(me_h * part, part), part)
    own_copy = pltpu.make_async_copy(
        kr_hbm.at[:, pl.ds(pl.multiple_of(me_h * width, width), width)], right.at[mine], own_sem)
    own_copy.start()
    di_copy.start()
    for c in fb_copies:
        c.start()

    barrier = pltpu.get_barrier_semaphore()
    for d in range(1, outer):
        pl.semaphore_signal(barrier, inc=1, device_id=(line(d), me_h), device_id_type=MESH)
    pl.semaphore_signal(barrier, inc=1, device_id=(across, me_h), device_id_type=MESH)
    for d in range(1, rhs):
        pl.semaphore_signal(barrier, inc=1, device_id=(me_r, lax.rem(me_h + d, rhs)), device_id_type=MESH)
    pl.semaphore_wait(barrier, outer - 1 + 1 + rhs - 1)

    kr_copies = []
    for d in range(1, rhs):
        peer = lax.rem(me_h + d, rhs)
        c = pltpu.make_async_remote_copy(
            src_ref=kr_hbm.at[:, pl.ds(pl.multiple_of(peer * width, width), width)],
            dst_ref=right.at[mine],
            send_sem=kr_send.at[d - 1], recv_sem=kr_recv.at[d - 1],
            device_id=(me_r, peer), device_id_type=MESH)
        c.start()
        kr_copies.append(c)

    def wait_rows(sender):
        @pl.when(me_h == sender)
        def _():
            own_copy.wait()

        for d in range(1, rhs):
            @pl.when(lax.rem(sender + d, rhs) == me_h)
            def _(d=d):
                kr_copies[d - 1].wait_recv()

    def send(lev, o, j, owner, target):
        ref = held[lev].at[owner, o]
        c = pltpu.make_async_remote_copy(
            src_ref=ref, dst_ref=ref,
            send_sem=x_send.at[lev, o, j], recv_sem=x_recv.at[lev, o, j],
            device_id=(target, me_h), device_id_type=MESH)
        c.start()
        return c

    started = []
    waited = 0
    near = sorted(range(1, outer), key=lambda d: min(d, outer - d))
    di_copy.wait()
    for lev in range(LEV):
        top = (lev + 1) * per_level * block
        while waited < rhs and waited * part < top:
            wait_rows(waited)
            waited += 1
        if lev:
            fb_copies[lev - 1].wait()
        direct = {}
        for o in range(per_level):
            s = lev * per_level + o
            at = pl.ds(s * block, block)
            residual = right[at]
            if lev:
                total = jnp.zeros((block, width), jnp.float32)
                for k in range(slots):
                    name = pat[s, k]
                    holder = name // per_device
                    local = name % per_device
                    of_level = local // per_level
                    offset = local % per_level
                    x = held[0][holder, offset]
                    for l in range(1, lev):
                        x = jnp.where(of_level == l, held[l][holder, offset], x)
                    x = jnp.where(k < live[s], x, jnp.zeros_like(x))
                    total += jnp.dot(factor[s - per_level, k], x, preferred_element_type=jnp.float32)
                residual = (residual.astype(jnp.float32) - total).astype(jnp.bfloat16)
            solved = jnp.dot(inverse[s], residual, preferred_element_type=jnp.float32).astype(jnp.bfloat16)
            out[at] = solved
            if lev + 1 < LEV:
                held[lev][me_r, o] = solved
                for d in near:
                    direct[o, d] = send(lev, o, d - 1, me_r, line(d))
                direct[o, 0] = send(lev, o, outer - 1, me_r, across)
        if lev + 1 < LEV:
            passed = []
            for d in near:
                for o in range(per_level):
                    direct[o, d].wait_recv()
                    passed.append(send(lev, o, outer - 1 + d, line(outer - d), across))
            for o in range(per_level):
                direct[o, 0].wait_recv()
            for c in passed:
                c.wait_recv()
            started += list(direct.values()) + passed
    for c in kr_copies + started:
        c.wait_send()


def shards(rows, rhs, kernel_rows, factor_blocks, diag_inverse, pattern, live_counts):
    per_device, slots, block, _ = factor_blocks.shape
    per_level = per_device // LEV
    width = kernel_rows.shape[1] // rhs
    kinds = 2 * (rows // 2) - 1
    bf = jnp.bfloat16
    any_spec = pl.BlockSpec(memory_space=pl.ANY)
    smem = pl.BlockSpec(memory_space=pltpu.SMEM)
    dma = pltpu.SemaphoreType.DMA
    return pl.pallas_call(
        functools.partial(kernel, rows, rhs),
        out_shape=jax.ShapeDtypeStruct((per_device * block, width), bf),
        in_specs=[any_spec, any_spec, any_spec, smem, smem],
        out_specs=pl.BlockSpec(memory_space=pltpu.VMEM),
        scratch_shapes=[
            pltpu.VMEM((per_device * block, width), bf),
            pltpu.VMEM((per_device - per_level, slots, block, block), bf),
            pltpu.VMEM((per_device, block, block), bf),
            *[pltpu.VMEM((rows, per_level, block, width), bf) for _ in range(LEV - 1)],
            dma((LEV - 1,)),
            dma,
            dma,
            dma((rhs - 1,)),
            dma((rhs - 1,)),
            dma((LEV - 1, per_level, kinds)),
            dma((LEV - 1, per_level, kinds)),
        ],
        compiler_params=pltpu.CompilerParams(
            collective_id=0, has_side_effects=True, vmem_limit_bytes=56 * 1024 * 1024
        ),
        cost_estimate=pl.CostEstimate(
            flops=2 * per_device * (slots + 1) * block * block * width,
            bytes_accessed=2 * per_device * slots * block * block,
            transcendentals=0,
        ),
    )(kernel_rows, factor_blocks, diag_inverse, pattern, live_counts)


def solution(mesh):
    placed = (
        P(("rows", "rhs"), None),
        P("rows", None, None, None),
        P("rows", None, None),
        P("rows", None),
        P("rows"),
    )
    body = functools.partial(shards, mesh.shape["rows"], mesh.shape["rhs"])
    return jax.shard_map(
        body, mesh=mesh, in_specs=placed, out_specs=P("rows", "rhs"), check_vma=False
    )
```

```python
import functools

import jax
import jax.numpy as jnp
from jax import lax
from jax.experimental import pallas as pl
from jax.experimental.pallas import tpu as pltpu
from jax.sharding import PartitionSpec as P

LEV = 4
MESH = pl.DeviceIdType.MESH


def kernel(rows, rhs, kr_hbm, fb_hbm, di_hbm, pat, live, out,
           right, factor, inverse, *rest):
    held = rest[: LEV - 1]
    fb_sem, di_sem, own_sem, kr_send, kr_recv, x_send, x_recv = rest[LEV - 1 :]
    per_device, slots, block, _ = fb_hbm.shape
    per_level = per_device // LEV
    width = out.shape[1]
    part = kr_hbm.shape[0]
    outer = rows // 2
    me_r = lax.axis_index("rows")
    me_h = lax.axis_index("rhs")
    z, y = me_r // 2, me_r % 2
    across = z * 2 + (1 - y)

    fb_copies = []
    for lev in range(1, LEV):
        at = pl.ds(lev * per_level, per_level)
        fb_copies.append(pltpu.make_async_copy(
            fb_hbm.at[at], factor.at[pl.ds((lev - 1) * per_level, per_level)], fb_sem.at[lev - 1]))
    di_copy = pltpu.make_async_copy(di_hbm, inverse, di_sem)
    mine = pl.ds(pl.multiple_of(me_h * part, part), part)
    own_copy = pltpu.make_async_copy(
        kr_hbm.at[:, pl.ds(pl.multiple_of(me_h * width, width), width)], right.at[mine], own_sem)
    own_copy.start()
    di_copy.start()
    for c in fb_copies:
        c.start()

    barrier = pltpu.get_barrier_semaphore()
    for d in (1, outer - 1):
        near = lax.rem(z + d, outer) * 2 + y
        pl.semaphore_signal(barrier, inc=1, device_id=(near, me_h), device_id_type=MESH)
    pl.semaphore_signal(barrier, inc=1, device_id=(across, me_h), device_id_type=MESH)
    for d in range(1, rhs):
        pl.semaphore_signal(barrier, inc=1, device_id=(me_r, lax.rem(me_h + d, rhs)), device_id_type=MESH)
    pl.semaphore_wait(barrier, 2 + 1 + rhs - 1)

    kr_copies = []
    for d in range(1, rhs):
        peer = lax.rem(me_h + d, rhs)
        c = pltpu.make_async_remote_copy(
            src_ref=kr_hbm.at[:, pl.ds(pl.multiple_of(peer * width, width), width)],
            dst_ref=right.at[mine],
            send_sem=kr_send.at[d - 1], recv_sem=kr_recv.at[d - 1],
            device_id=(me_r, peer), device_id_type=MESH)
        kr_copies.append(c)

    @pl.when(me_h == 0)
    def _():
        for c in kr_copies:
            c.start()

    def wait_rows(sender):
        @pl.when(me_h == sender)
        def _():
            own_copy.wait()

        for d in range(1, rhs):
            @pl.when(lax.rem(sender + d, rhs) == me_h)
            def _(d=d):
                kr_copies[d - 1].wait_recv()

    def copy(lev, o, owner, side, sent, landed, target):
        ref = held[lev].at[owner * 2 + side, o]
        return pltpu.make_async_remote_copy(
            src_ref=ref, dst_ref=ref,
            send_sem=x_send.at[lev, o, sent], recv_sem=x_recv.at[lev, o, landed],
            device_id=(target, me_h), device_id_type=MESH)

    def up(lev, o, owner):
        return copy(lev, o, owner, y, owner, owner, me_r + 2)

    def down(lev, o, owner):
        return copy(lev, o, owner, y, owner + 1, owner, me_r - 2)

    def over(lev, o, owner):
        return copy(lev, o, owner, y, outer + 1 + owner, outer + owner, across)

    def from_over(lev, o, owner):
        return copy(lev, o, owner, 1 - y, outer + 1 + owner, outer + owner, across)

    below, above = z > 0, z < outer - 1
    waited = 0
    di_copy.wait()
    for lev in range(LEV):
        top = (lev + 1) * per_level * block
        while waited < rhs and waited * part < top:
            wait_rows(waited)
            if waited == 0:
                @pl.when(me_h != 0)
                def _():
                    for c in kr_copies:
                        c.start()
            waited += 1
        if lev:
            fb_copies[lev - 1].wait()
        for o in range(per_level):
            s = lev * per_level + o
            at = pl.ds(s * block, block)
            residual = right[at]
            if lev:
                total = jnp.zeros((block, width), jnp.float32)
                for k in range(slots):
                    name = pat[s, k]
                    holder = name // per_device
                    local = name % per_device
                    of_level = local // per_level
                    offset = local % per_level
                    x = held[0][holder, offset]
                    for l in range(1, lev):
                        x = jnp.where(of_level == l, held[l][holder, offset], x)
                    x = jnp.where(k < live[s], x, jnp.zeros_like(x))
                    total += jnp.dot(factor[s - per_level, k], x, preferred_element_type=jnp.float32)
                residual = (residual.astype(jnp.float32) - total).astype(jnp.bfloat16)
            solved = jnp.dot(inverse[s], residual, preferred_element_type=jnp.float32).astype(jnp.bfloat16)
            out[at] = solved
            if lev + 1 < LEV:
                held[lev][me_r, o] = solved

                @pl.when(above)
                def _(o=o):
                    up(lev, o, z).start()

                @pl.when(below)
                def _(o=o):
                    down(lev, o, z).start()

                over(lev, o, z).start()
        if lev + 1 < LEV:
            for t in range(1, outer):
                for o in range(per_level):
                    @pl.when(z >= t)
                    def _(o=o, t=t):
                        up(lev, o, z - t).wait_recv()

                        @pl.when(above)
                        def _():
                            up(lev, o, z - t).start()

                        over(lev, o, z - t).start()

                    @pl.when(z + t < outer)
                    def _(o=o, t=t):
                        down(lev, o, z + t).wait_recv()

                        @pl.when(below)
                        def _():
                            down(lev, o, z + t).start()

                        over(lev, o, z + t).start()
            for owner in range(outer):
                for o in range(per_level):
                    from_over(lev, o, owner).wait_recv()
    for c in kr_copies:
        c.wait_send()
    for lev in range(LEV - 1):
        for o in range(per_level):
            for t in range(outer):
                @pl.when((z >= t) & above)
                def _(lev=lev, o=o, t=t):
                    up(lev, o, z - t).wait_send()

                @pl.when((z + t < outer) & below)
                def _(lev=lev, o=o, t=t):
                    down(lev, o, z + t).wait_send()

                over(lev, o, t).wait_send()


def shards(rows, rhs, kernel_rows, factor_blocks, diag_inverse, pattern, live_counts):
    per_device, slots, block, _ = factor_blocks.shape
    per_level = per_device // LEV
    width = kernel_rows.shape[1] // rhs
    outer = rows // 2
    bf = jnp.bfloat16
    any_spec = pl.BlockSpec(memory_space=pl.ANY)
    smem = pl.BlockSpec(memory_space=pltpu.SMEM)
    dma = pltpu.SemaphoreType.DMA
    return pl.pallas_call(
        functools.partial(kernel, rows, rhs),
        out_shape=jax.ShapeDtypeStruct((per_device * block, width), bf),
        in_specs=[any_spec, any_spec, any_spec, smem, smem],
        out_specs=pl.BlockSpec(memory_space=pltpu.VMEM),
        scratch_shapes=[
            pltpu.VMEM((per_device * block, width), bf),
            pltpu.VMEM((per_device - per_level, slots, block, block), bf),
            pltpu.VMEM((per_device, block, block), bf),
            *[pltpu.VMEM((rows, per_level, block, width), bf) for _ in range(LEV - 1)],
            dma((LEV - 1,)),
            dma,
            dma,
            dma((rhs - 1,)),
            dma((rhs - 1,)),
            dma((LEV - 1, per_level, 2 * outer + 1)),
            dma((LEV - 1, per_level, 2 * outer)),
        ],
        compiler_params=pltpu.CompilerParams(
            collective_id=0, has_side_effects=True, vmem_limit_bytes=56 * 1024 * 1024
        ),
        cost_estimate=pl.CostEstimate(
            flops=2 * per_device * (slots + 1) * block * block * width,
            bytes_accessed=2 * per_device * slots * block * block,
            transcendentals=0,
        ),
    )(kernel_rows, factor_blocks, diag_inverse, pattern, live_counts)


def solution(mesh):
    placed = (
        P(("rows", "rhs"), None),
        P("rows", None, None, None),
        P("rows", None, None),
        P("rows", None),
        P("rows"),
    )
    body = functools.partial(shards, mesh.shape["rows"], mesh.shape["rhs"])
    return jax.shard_map(
        body, mesh=mesh, in_specs=placed, out_specs=P("rows", "rhs"), check_vma=False
    )
```

```python
import functools

import jax
import jax.numpy as jnp
from jax import lax
from jax.experimental import pallas as pl
from jax.experimental.pallas import tpu as pltpu
from jax.sharding import PartitionSpec as P

LEV = 4
MESH = pl.DeviceIdType.MESH


def kernel(rows, rhs, kr_hbm, fb_hbm, di_hbm, pat, live, out,
           right, factor, inverse, *rest):
    held = rest[: LEV - 1]
    fb_sem, di_sem, own_sem, kr_send, kr_recv, x_send, x_recv = rest[LEV - 1 :]
    per_device, slots, block, _ = fb_hbm.shape
    per_level = per_device // LEV
    width = out.shape[1]
    part = kr_hbm.shape[0]
    outer = rows // 2
    me_r = lax.axis_index("rows")
    me_h = lax.axis_index("rhs")
    z, y = me_r // 2, me_r % 2
    across = z * 2 + (1 - y)

    fb_copies = []
    for lev in range(1, LEV):
        at = pl.ds(lev * per_level, per_level)
        fb_copies.append(pltpu.make_async_copy(
            fb_hbm.at[at], factor.at[pl.ds((lev - 1) * per_level, per_level)], fb_sem.at[lev - 1]))
    di_copy = pltpu.make_async_copy(di_hbm, inverse, di_sem)
    mine = pl.ds(pl.multiple_of(me_h * part, part), part)
    own_copy = pltpu.make_async_copy(
        kr_hbm.at[:, pl.ds(pl.multiple_of(me_h * width, width), width)], right.at[mine], own_sem)
    own_copy.start()
    di_copy.start()
    for c in fb_copies:
        c.start()

    barrier = pltpu.get_barrier_semaphore()
    for d in (1, outer - 1):
        near = lax.rem(z + d, outer) * 2 + y
        pl.semaphore_signal(barrier, inc=1, device_id=(near, me_h), device_id_type=MESH)
    pl.semaphore_signal(barrier, inc=1, device_id=(across, me_h), device_id_type=MESH)
    for d in range(1, rhs):
        pl.semaphore_signal(barrier, inc=1, device_id=(me_r, lax.rem(me_h + d, rhs)), device_id_type=MESH)
    pl.semaphore_wait(barrier, 2 + 1 + rhs - 1)

    kr_copies = []
    for d in range(1, rhs):
        peer = lax.rem(me_h + d, rhs)
        c = pltpu.make_async_remote_copy(
            src_ref=kr_hbm.at[:, pl.ds(pl.multiple_of(peer * width, width), width)],
            dst_ref=right.at[mine],
            send_sem=kr_send.at[d - 1], recv_sem=kr_recv.at[d - 1],
            device_id=(me_r, peer), device_id_type=MESH)
        kr_copies.append(c)

    @pl.when(me_h == 0)
    def _():
        for c in kr_copies:
            c.start()

    def wait_rows(sender):
        @pl.when(me_h == sender)
        def _():
            own_copy.wait()

        for d in range(1, rhs):
            @pl.when(lax.rem(sender + d, rhs) == me_h)
            def _(d=d):
                kr_copies[d - 1].wait_recv()

    first = block - block * 3 // 16
    whole, head, tail = (0, block), (0, first), (first, block - first)

    def copy(lev, o, owner, side, span, sent, landed, target):
        ref = held[lev].at[owner * 2 + side, o, pl.ds(*span)]
        return pltpu.make_async_remote_copy(
            src_ref=ref, dst_ref=ref,
            send_sem=x_send.at[lev, o, sent], recv_sem=x_recv.at[lev, o, landed],
            device_id=(target, me_h), device_id_type=MESH)

    def up(lev, o, owner):
        return copy(lev, o, owner, y, whole, owner, owner, me_r + 2)

    def down(lev, o, owner):
        return copy(lev, o, owner, y, whole, owner + 1, owner, me_r - 2)

    def up_tail(lev, o, owner):
        return copy(lev, o, owner, 1 - y, tail, 2 * outer + 1 + owner, 2 * outer + owner, me_r + 2)

    def down_tail(lev, o, owner):
        return copy(lev, o, owner, 1 - y, tail, 2 * outer + 2 + owner, 2 * outer + owner, me_r - 2)

    def over(lev, o, owner, span=head):
        return copy(lev, o, owner, y, span, outer + 1 + owner, outer + owner, across)

    def from_over(lev, o, owner, span=head):
        return copy(lev, o, owner, 1 - y, span, outer + 1 + owner, outer + owner, across)

    below, above = z > 0, z < outer - 1
    waited = 0
    di_copy.wait()
    for lev in range(LEV):
        top = (lev + 1) * per_level * block
        while waited < rhs and waited * part < top:
            wait_rows(waited)
            if waited == 0:
                @pl.when(me_h != 0)
                def _():
                    for c in kr_copies:
                        c.start()
            waited += 1
        if lev:
            fb_copies[lev - 1].wait()
        for o in range(per_level):
            s = lev * per_level + o
            at = pl.ds(s * block, block)
            residual = right[at]
            if lev:
                total = jnp.zeros((block, width), jnp.float32)
                for k in range(slots):
                    name = pat[s, k]
                    holder = name // per_device
                    local = name % per_device
                    of_level = local // per_level
                    offset = local % per_level
                    x = held[0][holder, offset]
                    for l in range(1, lev):
                        x = jnp.where(of_level == l, held[l][holder, offset], x)
                    x = jnp.where(k < live[s], x, jnp.zeros_like(x))
                    total += jnp.dot(factor[s - per_level, k], x, preferred_element_type=jnp.float32)
                residual = (residual.astype(jnp.float32) - total).astype(jnp.bfloat16)
            solved = jnp.dot(inverse[s], residual, preferred_element_type=jnp.float32).astype(jnp.bfloat16)
            out[at] = solved
            if lev + 1 < LEV:
                held[lev][me_r, o] = solved

                @pl.when(above)
                def _(o=o):
                    up(lev, o, z).start()

                @pl.when(below)
                def _(o=o):
                    down(lev, o, z).start()

                over(lev, o, z, whole).start()
        if lev + 1 < LEV:
            for t in range(1, outer):
                for o in range(per_level):
                    @pl.when(z >= t)
                    def _(o=o, t=t):
                        up(lev, o, z - t).wait_recv()

                        @pl.when(above)
                        def _():
                            up(lev, o, z - t).start()

                        over(lev, o, z - t).start()

                    @pl.when(z + t < outer)
                    def _(o=o, t=t):
                        down(lev, o, z + t).wait_recv()

                        @pl.when(below)
                        def _():
                            down(lev, o, z + t).start()

                        over(lev, o, z + t).start()
                for o in range(per_level):
                    if t == 1:
                        from_over(lev, o, z, whole).wait_recv()

                        @pl.when(above)
                        def _(o=o):
                            up_tail(lev, o, z).start()

                        @pl.when(below)
                        def _(o=o):
                            down_tail(lev, o, z).start()
                for o in range(per_level):
                    @pl.when(z >= t)
                    def _(o=o, t=t):
                        up_tail(lev, o, z - t).wait_recv()

                        @pl.when(above)
                        def _():
                            up_tail(lev, o, z - t).start()

                    @pl.when(z + t < outer)
                    def _(o=o, t=t):
                        down_tail(lev, o, z + t).wait_recv()

                        @pl.when(below)
                        def _():
                            down_tail(lev, o, z + t).start()
            for t in range(1, outer):
                for o in range(per_level):
                    from_over(lev, o, lax.rem(z + t, outer)).wait_recv()
    for c in kr_copies:
        c.wait_send()
    for lev in range(LEV - 1):
        for o in range(per_level):
            for t in range(outer):
                @pl.when((z >= t) & above)
                def _(lev=lev, o=o, t=t):
                    up(lev, o, z - t).wait_send()
                    up_tail(lev, o, z - t).wait_send()

                @pl.when((z + t < outer) & below)
                def _(lev=lev, o=o, t=t):
                    down(lev, o, z + t).wait_send()
                    down_tail(lev, o, z + t).wait_send()

                over(lev, o, lax.rem(z + t, outer), head if t else whole).wait_send()


def shards(rows, rhs, kernel_rows, factor_blocks, diag_inverse, pattern, live_counts):
    per_device, slots, block, _ = factor_blocks.shape
    per_level = per_device // LEV
    width = kernel_rows.shape[1] // rhs
    outer = rows // 2
    bf = jnp.bfloat16
    any_spec = pl.BlockSpec(memory_space=pl.ANY)
    smem = pl.BlockSpec(memory_space=pltpu.SMEM)
    dma = pltpu.SemaphoreType.DMA
    return pl.pallas_call(
        functools.partial(kernel, rows, rhs),
        out_shape=jax.ShapeDtypeStruct((per_device * block, width), bf),
        in_specs=[any_spec, any_spec, any_spec, smem, smem],
        out_specs=pl.BlockSpec(memory_space=pltpu.VMEM),
        scratch_shapes=[
            pltpu.VMEM((per_device * block, width), bf),
            pltpu.VMEM((per_device - per_level, slots, block, block), bf),
            pltpu.VMEM((per_device, block, block), bf),
            *[pltpu.VMEM((rows, per_level, block, width), bf) for _ in range(LEV - 1)],
            dma((LEV - 1,)),
            dma,
            dma,
            dma((rhs - 1,)),
            dma((rhs - 1,)),
            dma((LEV - 1, per_level, 3 * outer + 2)),
            dma((LEV - 1, per_level, 3 * outer)),
        ],
        compiler_params=pltpu.CompilerParams(
            collective_id=0, has_side_effects=True, vmem_limit_bytes=56 * 1024 * 1024
        ),
        cost_estimate=pl.CostEstimate(
            flops=2 * per_device * (slots + 1) * block * block * width,
            bytes_accessed=2 * per_device * slots * block * block,
            transcendentals=0,
        ),
    )(kernel_rows, factor_blocks, diag_inverse, pattern, live_counts)


def solution(mesh):
    placed = (
        P(("rows", "rhs"), None),
        P("rows", None, None, None),
        P("rows", None, None),
        P("rows", None),
        P("rows"),
    )
    body = functools.partial(shards, mesh.shape["rows"], mesh.shape["rhs"])
    return jax.shard_map(
        body, mesh=mesh, in_specs=placed, out_specs=P("rows", "rhs"), check_vma=False
    )
```

```python
import functools

import jax
import jax.numpy as jnp
from jax import lax
from jax.experimental import pallas as pl
from jax.experimental.pallas import tpu as pltpu
from jax.sharding import PartitionSpec as P

LEV = 4
MESH = pl.DeviceIdType.MESH


def kernel(rows, rhs, kr_hbm, fb_hbm, di_hbm, pat, live, out,
           right, factor, inverse, *rest):
    held = rest[: LEV - 1]
    fb_sem, di_sem, own_sem, kr_send, kr_recv, x_send, x_recv = rest[LEV - 1 :]
    per_device, slots, block, _ = fb_hbm.shape
    per_level = per_device // LEV
    width = out.shape[1]
    part = kr_hbm.shape[0]
    outer = rows // 2
    me_r = lax.axis_index("rows")
    me_h = lax.axis_index("rhs")
    z, y = me_r // 2, me_r % 2
    across = z * 2 + (1 - y)

    fb_copies = []
    for lev in range(1, LEV):
        at = pl.ds(lev * per_level, per_level)
        fb_copies.append(pltpu.make_async_copy(
            fb_hbm.at[at], factor.at[pl.ds((lev - 1) * per_level, per_level)], fb_sem.at[lev - 1]))
    di_copy = pltpu.make_async_copy(di_hbm, inverse, di_sem)
    mine = pl.ds(pl.multiple_of(me_h * part, part), part)
    own_copy = pltpu.make_async_copy(
        kr_hbm.at[:, pl.ds(pl.multiple_of(me_h * width, width), width)], right.at[mine], own_sem)
    own_copy.start()
    di_copy.start()
    for c in fb_copies:
        c.start()

    barrier = pltpu.get_barrier_semaphore()
    for d in (1, outer - 1):
        near = lax.rem(z + d, outer) * 2 + y
        pl.semaphore_signal(barrier, inc=1, device_id=(near, me_h), device_id_type=MESH)
    pl.semaphore_signal(barrier, inc=1, device_id=(across, me_h), device_id_type=MESH)
    for d in range(1, rhs):
        pl.semaphore_signal(barrier, inc=1, device_id=(me_r, lax.rem(me_h + d, rhs)), device_id_type=MESH)
    pl.semaphore_wait(barrier, 2 + 1 + rhs - 1)

    kr_copies = []
    for d in range(1, rhs):
        peer = lax.rem(me_h + d, rhs)
        c = pltpu.make_async_remote_copy(
            src_ref=kr_hbm.at[:, pl.ds(pl.multiple_of(peer * width, width), width)],
            dst_ref=right.at[mine],
            send_sem=kr_send.at[d - 1], recv_sem=kr_recv.at[d - 1],
            device_id=(me_r, peer), device_id_type=MESH)
        kr_copies.append(c)

    @pl.when(me_h == 0)
    def _():
        for c in kr_copies:
            c.start()

    def wait_rows(sender):
        @pl.when(me_h == sender)
        def _():
            own_copy.wait()

        for d in range(1, rhs):
            @pl.when(lax.rem(sender + d, rhs) == me_h)
            def _(d=d):
                kr_copies[d - 1].wait_recv()

    sub = 2
    share = block // sub

    def copy(lev, o, owner, side, sent, landed, target):
        ref = held[lev].at[owner * 2 + side, o // sub, pl.ds(o % sub * share, share)]
        return pltpu.make_async_remote_copy(
            src_ref=ref, dst_ref=ref,
            send_sem=x_send.at[lev, o, sent], recv_sem=x_recv.at[lev, o, landed],
            device_id=(target, me_h), device_id_type=MESH)

    def up(lev, o, owner):
        return copy(lev, o, owner, y, owner, owner, me_r + 2)

    def down(lev, o, owner):
        return copy(lev, o, owner, y, owner + 1, owner, me_r - 2)

    def over(lev, o, owner):
        return copy(lev, o, owner, y, outer + 1 + owner, outer + owner, across)

    def from_over(lev, o, owner):
        return copy(lev, o, owner, 1 - y, outer + 1 + owner, outer + owner, across)

    below, above = z > 0, z < outer - 1
    waited = 0
    di_copy.wait()
    for lev in range(LEV):
        top = (lev + 1) * per_level * block
        while waited < rhs and waited * part < top:
            wait_rows(waited)
            if waited == 0:
                @pl.when(me_h != 0)
                def _():
                    for c in kr_copies:
                        c.start()
            waited += 1
        if lev:
            fb_copies[lev - 1].wait()
        for o in range(per_level):
            s = lev * per_level + o
            at = pl.ds(s * block, block)
            residual = right[at]
            if lev:
                total = jnp.zeros((block, width), jnp.float32)
                for k in range(slots):
                    name = pat[s, k]
                    holder = name // per_device
                    local = name % per_device
                    of_level = local // per_level
                    offset = local % per_level
                    x = held[0][holder, offset]
                    for l in range(1, lev):
                        x = jnp.where(of_level == l, held[l][holder, offset], x)
                    x = jnp.where(k < live[s], x, jnp.zeros_like(x))
                    total += jnp.dot(factor[s - per_level, k], x, preferred_element_type=jnp.float32)
                residual = (residual.astype(jnp.float32) - total).astype(jnp.bfloat16)
            solved = jnp.dot(inverse[s], residual, preferred_element_type=jnp.float32).astype(jnp.bfloat16)
            out[at] = solved
            if lev + 1 < LEV:
                held[lev][me_r, o] = solved

                for o in range(o * sub, (o + 1) * sub):
                    @pl.when(above)
                    def _(o=o):
                        up(lev, o, z).start()

                    @pl.when(below)
                    def _(o=o):
                        down(lev, o, z).start()

                    over(lev, o, z).start()
        if lev + 1 < LEV:
            for t in range(1, outer):
                for o in range(per_level * sub):
                    @pl.when(z >= t)
                    def _(o=o, t=t):
                        up(lev, o, z - t).wait_recv()

                        @pl.when(above)
                        def _():
                            up(lev, o, z - t).start()

                        over(lev, o, z - t).start()

                    @pl.when(z + t < outer)
                    def _(o=o, t=t):
                        down(lev, o, z + t).wait_recv()

                        @pl.when(below)
                        def _():
                            down(lev, o, z + t).start()

                        over(lev, o, z + t).start()
            for owner in range(outer):
                for o in range(per_level * sub):
                    from_over(lev, o, owner).wait_recv()
    for c in kr_copies:
        c.wait_send()
    for lev in range(LEV - 1):
        for o in range(per_level * sub):
            for t in range(outer):
                @pl.when((z >= t) & above)
                def _(lev=lev, o=o, t=t):
                    up(lev, o, z - t).wait_send()

                @pl.when((z + t < outer) & below)
                def _(lev=lev, o=o, t=t):
                    down(lev, o, z + t).wait_send()

                over(lev, o, t).wait_send()


def shards(rows, rhs, kernel_rows, factor_blocks, diag_inverse, pattern, live_counts):
    per_device, slots, block, _ = factor_blocks.shape
    per_level = per_device // LEV
    width = kernel_rows.shape[1] // rhs
    outer = rows // 2
    bf = jnp.bfloat16
    any_spec = pl.BlockSpec(memory_space=pl.ANY)
    smem = pl.BlockSpec(memory_space=pltpu.SMEM)
    dma = pltpu.SemaphoreType.DMA
    return pl.pallas_call(
        functools.partial(kernel, rows, rhs),
        out_shape=jax.ShapeDtypeStruct((per_device * block, width), bf),
        in_specs=[any_spec, any_spec, any_spec, smem, smem],
        out_specs=pl.BlockSpec(memory_space=pltpu.VMEM),
        scratch_shapes=[
            pltpu.VMEM((per_device * block, width), bf),
            pltpu.VMEM((per_device - per_level, slots, block, block), bf),
            pltpu.VMEM((per_device, block, block), bf),
            *[pltpu.VMEM((rows, per_level, block, width), bf) for _ in range(LEV - 1)],
            dma((LEV - 1,)),
            dma,
            dma,
            dma((rhs - 1,)),
            dma((rhs - 1,)),
            dma((LEV - 1, per_level * 2, 2 * outer + 1)),
            dma((LEV - 1, per_level * 2, 2 * outer)),
        ],
        compiler_params=pltpu.CompilerParams(
            collective_id=0, has_side_effects=True, vmem_limit_bytes=56 * 1024 * 1024
        ),
        cost_estimate=pl.CostEstimate(
            flops=2 * per_device * (slots + 1) * block * block * width,
            bytes_accessed=2 * per_device * slots * block * block,
            transcendentals=0,
        ),
    )(kernel_rows, factor_blocks, diag_inverse, pattern, live_counts)


def solution(mesh):
    placed = (
        P(("rows", "rhs"), None),
        P("rows", None, None, None),
        P("rows", None, None),
        P("rows", None),
        P("rows"),
    )
    body = functools.partial(shards, mesh.shape["rows"], mesh.shape["rhs"])
    return jax.shard_map(
        body, mesh=mesh, in_specs=placed, out_specs=P("rows", "rhs"), check_vma=False
    )
```
